32 devices in a mesh: gr: 8 (over y, x, core), gc: 4 (over z).
Axes of the slice: x: 2, y: 2, z: 4, core: 2. Of those that a mesh axis runs over, the one named last changes fastest.
Arguments:
- features: bfloat16 [4, 8, 512, 128], P('gc', 'gr'), may hold values from -6 to 6
- out_grad: bfloat16 [8, 4, 512, 128], P('gr', 'gc'), may hold values from -6 to 6
- weight: bfloat16 [128, 128], replicated, may hold values from -0.5 to 0.5
- block_values: bfloat16 [8, 4, 128, 128, 128], P('gr', 'gc'), may hold values from 0 to 0.03491211
- block_slot: int32 [8, 4, 128], P('gr', 'gc'), may hold values from 0 to 127, as said below
- live_count: int32 [8, 4], P('gr', 'gc'), may hold values from 32 to 128, as said below
- row_need: int32 [8, 4, 4, 2], P('gr', 'gc'), may hold values from 0 to 3, as said below
- col_need: int32 [8, 4, 8, 2], P('gr', 'gc'), may hold values from 0 to 3, as said below
Outputs:
- activated: bfloat16 [8, 4, 512, 128], P('gr', 'gc')
- weight_grad: float32 [128, 128], replicated
- input_grad: bfloat16 [4, 8, 512, 128], P('gc', 'gr')
The draws below stay inside these ranges and needn't reach their ends.
Inputs may be any that keep to these rules, and one draw needn't show every extreme that they name: `block_slot`: within one tile the 128 entries are distinct. `live_count`: each tile holds 128, 64 or 32 live slots; some tile holds 128 in every draw. `row_need`: the 2 entries for one tile and one owner are distinct. `col_need`: the 2 entries for one tile and one owner are distinct.
All inputs are finite; a program needn't handle non-finite values.
Results may differ from the reference program's by a relative error of at most 0.0069.
Values may be sent and summed in bfloat16 or wider, within the bound.
A program may use at most 64 MiB of HBM per device.

```python
import jax
import jax.numpy as jnp
from jax import lax

F = 128
BLK = 128
NL = 512
NZB = 128
CAP = 2
NODES = 16384
N_GR = 8
N_GC = 4


def distinct_pick(key, lead, total, keep):
    scores = jax.random.randint(key, lead + (total,), 0, 2 ** 30 // total) * total + jnp.arange(total)
    return jnp.argsort(scores, axis=-1)[..., :keep].astype(jnp.int32)


def draw_block_slot(key, part):
    slot_total = N_GC * CAP * N_GR * CAP
    return distinct_pick(jax.random.fold_in(key, 11), (N_GR, N_GC), slot_total, NZB)


def draw_row_need(key, part):
    return distinct_pick(jax.random.fold_in(key, 12), (N_GR, N_GC, N_GC), NL // BLK, CAP)


def draw_col_need(key, part):
    return distinct_pick(jax.random.fold_in(key, 13), (N_GR, N_GC, N_GR), NL // BLK, CAP)


def draw_live_count(key, part):
    levels = jax.random.randint(jax.random.fold_in(key, 14), (N_GR * N_GC,), 0, 3)
    divisor = jnp.where(levels == 0, 1, jnp.where(levels == 1, 2, 4))
    counts = NZB // divisor
    fullest = jax.random.randint(jax.random.fold_in(key, 15), (), 0, N_GR * N_GC)
    counts = jnp.where(jnp.arange(N_GR * N_GC) == fullest, NZB, counts)
    return counts.reshape(N_GR, N_GC).astype(jnp.int32)


def level_of(key, dims, cuts, low, top_value):
    loudness, own = 1.0, jax.random.fold_in(key, 6)
    for dim, parts in cuts:
        steps = jnp.exp(jax.random.uniform(jax.random.fold_in(own, dim), (parts,), jnp.float32, low / len(cuts), top_value / len(cuts)))
        loudness = loudness * jnp.repeat(steps, dims[dim] // parts).reshape([-1 if axis == dim else 1 for axis in range(len(dims))])
    return loudness


def scatter_about(key, shape, scale, reach, pieces=(), held_as=jnp.bfloat16):
    level = level_of(key, shape, pieces, -0.22, 0.18) if pieces else 1.0
    result = jax.random.normal(key, shape, jnp.float32) * scale * level
    return jnp.minimum(jnp.maximum(result, -reach), reach).astype(held_as)


def setup_inputs(seed: int = 0) -> dict:
    arg_keys = jax.random.split(jax.random.key(seed), 9)
    return {
        "features": scatter_about(arg_keys[0], (N_GC, N_GR, NL, F), 1.0, 6.0, ((0, 4), (1, 8))),
        "out_grad": scatter_about(arg_keys[1], (N_GR, N_GC, NL, F), 1.0, 6.0, ((0, 8), (1, 4))),
        "weight": scatter_about(arg_keys[2], (F, F), F ** -0.5, 0.5),
        "block_values": jnp.clip(0.03491211 * jax.random.uniform(arg_keys[3], (N_GR, N_GC, NZB, BLK, BLK), jnp.float32) ** level_of(arg_keys[3], (N_GR, N_GC, NZB, BLK, BLK), ((0, 8), (1, 4)), -0.2, 0.2), 0.0, 0.03491211).astype(jnp.bfloat16),
        "block_slot": draw_block_slot(jax.random.fold_in(arg_keys[8], 71), 0),
        "live_count": draw_live_count(jax.random.fold_in(arg_keys[8], 71), 0),
        "row_need": draw_row_need(jax.random.fold_in(arg_keys[8], 71), 0),
        "col_need": draw_col_need(jax.random.fold_in(arg_keys[8], 71), 0),
    }


def reference(features, out_grad, weight, block_values, block_slot, live_count, row_need, col_need):
    per_dev = NL // BLK
    col_slots = N_GR * CAP
    row_slots = N_GC * CAP
    feature_blocks = features.reshape(N_GC, N_GR, per_dev, BLK, F)

    def forward_tile(tile, accum):
        i = tile // N_GC
        j = tile % N_GC
        values = block_values[i, j].astype(jnp.float32)
        slots = block_slot[i, j]
        live = (jnp.arange(NZB) < live_count[i, j]).astype(jnp.float32)
        row_of = slots // col_slots
        col_of = slots % col_slots
        picked = feature_blocks[j][jnp.arange(N_GR)[:, None], col_need[i, j]]
        picked = picked.reshape(col_slots, BLK, F).astype(jnp.float32)
        terms = jnp.einsum("bmk,bkf->bmf", values, picked[col_of]) * live[:, None, None]
        partial_value = jax.ops.segment_sum(terms, row_of, num_segments=row_slots).astype(jnp.bfloat16)
        partial_value = lax.optimization_barrier(partial_value).astype(jnp.float32)
        owners = jnp.arange(row_slots) // CAP
        blocks = row_need[i, j].reshape(-1)
        return accum.at[i, owners, blocks].add(partial_value)

    start = jnp.zeros((N_GR, N_GC, per_dev, BLK, F), jnp.float32)
    accum = lax.fori_loop(0, N_GR * N_GC, forward_tile, start)
    aggregated = accum.astype(jnp.bfloat16).reshape(-1, F)
    pre = jnp.dot(aggregated, weight, preferred_element_type=jnp.float32)
    sig = jax.nn.sigmoid(pre)
    activated = (pre * sig).astype(jnp.bfloat16)
    upstream = out_grad.reshape(-1, F).astype(jnp.float32)
    grad_pre = (upstream * sig * (1.0 + pre * (1.0 - sig))).astype(jnp.bfloat16)
    weight_grad = jnp.dot(aggregated.T, grad_pre, preferred_element_type=jnp.float32) * (float(NODES) ** -0.5)
    back_rows = jnp.dot(grad_pre, weight.T, preferred_element_type=jnp.float32).astype(jnp.bfloat16)
    back_blocks = back_rows.reshape(N_GR, N_GC, per_dev, BLK, F)

    def backward_tile(tile, accum):
        i = tile // N_GC
        j = tile % N_GC
        values = block_values[i, j].astype(jnp.float32)
        slots = block_slot[i, j]
        live = (jnp.arange(NZB) < live_count[i, j]).astype(jnp.float32)
        row_of = slots // col_slots
        col_of = slots % col_slots
        picked = back_blocks[i][jnp.arange(N_GC)[:, None], row_need[i, j]]
        picked = picked.reshape(row_slots, BLK, F).astype(jnp.float32)
        terms = jnp.einsum("bmk,bmf->bkf", values, picked[row_of]) * live[:, None, None]
        partial_value = jax.ops.segment_sum(terms, col_of, num_segments=col_slots).astype(jnp.bfloat16)
        partial_value = lax.optimization_barrier(partial_value).astype(jnp.float32)
        sources = jnp.arange(col_slots) // CAP
        blocks = col_need[i, j].reshape(-1)
        return accum.at[j, sources, blocks].add(partial_value)

    start_back = jnp.zeros((N_GC, N_GR, per_dev, BLK, F), jnp.float32)
    accum_back = lax.fori_loop(0, N_GR * N_GC, backward_tile, start_back)
    input_grad = accum_back.astype(jnp.bfloat16).reshape(N_GC, N_GR, NL, F)
    return activated.reshape(N_GR, N_GC, NL, F), weight_grad, input_grad
```

```python
import functools

import jax
import jax.numpy as jnp
from jax import lax
from jax.experimental import pallas as pl
from jax.experimental.pallas import tpu as pltpu
from jax.sharding import PartitionSpec as P

MESH = pl.DeviceIdType.MESH


def kernel(
    n_rows,
    n_cols,
    cap,
    scale,
    inv,
    col_need,
    row_meta,
    col_meta,
    features,
    out_grad,
    weight,
    values,
    activated,
    weight_grad,
    input_grad,
    vals,
    gathered,
    picked,
    part_out,
    part_in,
    agg,
    back,
    back_out,
    back_in,
    dx_out,
    dx_in,
    row_vm,
    col_vm,
    row_sm,
    col_sm,
    wg_out,
    wg_in,
    wg_piece,
    wg_part,
    wg_done,
    local_sem,
    row_meta_s,
    row_meta_r,
    col_meta_s,
    col_meta_r,
    feat_s,
    feat_r,
    part_s,
    part_r,
    back_s,
    back_r,
    dx_s,
    dx_r,
    wg1_s,
    wg1_r,
    wg2_s,
    wg2_r,
    wg3_s,
    wg3_r,
):
    r_me, c_me = lax.axis_index("gr"), lax.axis_index("gc")
    nzb, blk, _ = values.shape
    per_dev, _, width = features.shape
    col_slots, row_slots = n_rows * cap, n_cols * cap

    def row_at(d):
        return lax.rem(r_me + d, n_rows)

    def col_at(d):
        return lax.rem(c_me + d, n_cols)

    def to_row(d, src, dst, send, recv):
        return pltpu.make_async_remote_copy(
            src_ref=src,
            dst_ref=dst,
            send_sem=send.at[d],
            recv_sem=recv.at[d],
            device_id={"gr": row_at(d)},
            device_id_type=MESH,
        )

    def to_col(d, src, dst, send, recv):
        return pltpu.make_async_remote_copy(
            src_ref=src,
            dst_ref=dst,
            send_sem=send.at[d],
            recv_sem=recv.at[d],
            device_id={"gc": col_at(d)},
            device_id_type=MESH,
        )

    def each(n, body):
        def step(d, carry):
            body(d)
            return carry

        lax.fori_loop(1, n, step, 0)

    load_vals = pltpu.make_async_copy(values, vals.at[pl.ds(0, nzb)], local_sem.at[0])
    load_vals.start()
    mine = pl.ds(r_me * per_dev, per_dev)
    load_own = pltpu.make_async_copy(features, gathered.at[mine], local_sem.at[1])
    load_own.start()

    barrier = pltpu.get_barrier_semaphore()

    def greet_row(d):
        pl.semaphore_signal(barrier, inc=1, device_id={"gr": row_at(d)}, device_id_type=MESH)

    def greet_col(d):
        pl.semaphore_signal(barrier, inc=1, device_id={"gc": col_at(d)}, device_id_type=MESH)

    each(n_rows, greet_row)
    each(n_cols, greet_col)
    pl.semaphore_wait(barrier, n_rows + n_cols - 2)

    def feat_copy(d):
        return to_row(d, features, gathered.at[mine], feat_s, feat_r)

    def row_meta_copy(d):
        return to_col(d, row_meta, row_vm.at[c_me], row_meta_s, row_meta_r)

    def col_meta_copy(d):
        return to_row(d, col_meta, col_vm.at[r_me], col_meta_s, col_meta_r)

    each(n_cols, lambda d: row_meta_copy(d).start())
    each(n_rows, lambda d: col_meta_copy(d).start())
    each(n_rows, lambda d: feat_copy(d).start())

    zero = jnp.zeros((blk, width), jnp.bfloat16)
    vals[nzb] = jnp.zeros((blk, blk), jnp.bfloat16)
    part_in[row_slots] = zero
    dx_in[col_slots] = zero
    row_vm[c_me] = row_meta[...]
    col_vm[r_me] = col_meta[...]

    each(n_cols, lambda d: row_meta_copy(d).wait())
    each(n_rows, lambda d: col_meta_copy(d).wait())
    row_load = pltpu.make_async_copy(row_vm, row_sm, local_sem.at[2])
    col_load = pltpu.make_async_copy(col_vm, col_sm, local_sem.at[3])
    row_load.start()
    col_load.start()
    load_own.wait()
    load_vals.wait()
    each(n_rows, lambda d: feat_copy(d).wait())
    row_load.wait()
    col_load.wait()

    for s in range(col_slots):
        picked[pl.ds(s * blk, blk), :] = gathered[s // cap * per_dev + col_need[s // cap, s % cap]]

    def forward(t):
        left = jnp.concatenate([vals[inv[t * col_slots + s]] for s in range(col_slots)], axis=1)
        total = jnp.dot(left, picked[...], preferred_element_type=jnp.float32)
        return total.astype(jnp.bfloat16)

    def part_copy(d):
        c = col_at(d)
        return to_col(
            d,
            part_out.at[pl.ds(c * cap, cap)],
            part_in.at[pl.ds(c_me * cap, cap)],
            part_s,
            part_r,
        )

    def forward_to(d):
        for k in range(cap):
            part_out[col_at(d) * cap + k] = forward(col_at(d) * cap + k)
        part_copy(d).start()

    each(n_cols, forward_to)
    for k in range(cap):
        part_in[c_me * cap + k] = forward(c_me * cap + k)
    each(n_cols, lambda d: part_copy(d).wait())

    def total_of(ref, asked, n, k):
        total = jnp.zeros((blk, width), jnp.float32)
        for o in range(n):
            place = n * cap
            for q in range(cap):
                place = jnp.where(asked[o][q] == k, o * cap + q, place)
            total = total + ref[place].astype(jnp.float32)
        return total.astype(jnp.bfloat16)

    row_asked = [[row_sm[o, 0, c_me * cap + q] for q in range(cap)] for o in range(n_cols)]
    for k in range(per_dev):
        agg[pl.ds(k * blk, blk), :] = total_of(part_in, row_asked, n_cols, k)
    held = agg[...]
    pre = jnp.dot(held, weight[...], preferred_element_type=jnp.float32)
    sig = jax.nn.sigmoid(pre)
    activated[...] = (pre * sig).astype(jnp.bfloat16)
    upstream = out_grad[...].astype(jnp.float32)
    grad_pre = (upstream * sig * (1.0 + pre * (1.0 - sig))).astype(jnp.bfloat16)
    rows = lax.dot_general(
        grad_pre, weight[...], (((1,), (1,)), ((), ())), preferred_element_type=jnp.float32
    ).astype(jnp.bfloat16)
    for k in range(per_dev):
        back[k] = rows[k * blk : (k + 1) * blk]

    def back_copy(d):
        c = col_at(d)
        return to_col(
            d,
            back_out.at[pl.ds(c * cap, cap)],
            back_in.at[pl.ds(c_me * cap, cap)],
            back_s,
            back_r,
        )

    def back_to(d):
        c = col_at(d)
        for k in range(cap):
            back_out[c * cap + k] = back[row_sm[c, 0, c_me * cap + k]]
        back_copy(d).start()

    each(n_cols, back_to)
    for k in range(cap):
        back_in[c_me * cap + k] = back[row_sm[c_me, 0, c_me * cap + k]]

    term = lax.dot_general(
        held, grad_pre, (((0,), (0,)), ((), ())), preferred_element_type=jnp.float32
    )
    piece = term.shape[0] // n_rows
    for o in range(n_rows):
        wg_out[o] = term[o * piece : (o + 1) * piece]
    wg_in[r_me] = wg_out[r_me]

    def wg1_copy(d):
        return to_row(d, wg_out.at[row_at(d)], wg_in.at[r_me], wg1_s, wg1_r)

    def wg2_copy(d):
        return to_col(d, wg_piece, wg_part.at[c_me], wg2_s, wg2_r)

    def wg3_copy(d):
        return to_row(d, wg_piece3, wg_done.at[r_me], wg3_s, wg3_r)

    wg_piece3 = wg_out.at[0]

    each(n_rows, lambda d: wg1_copy(d).start())
    each(n_cols, lambda d: back_copy(d).wait())
    each(n_rows, lambda d: wg1_copy(d).wait())
    total = wg_in[0]
    for o in range(1, n_rows):
        total = total + wg_in[o]
    wg_piece[...] = total
    wg_part[c_me] = total
    each(n_cols, lambda d: wg2_copy(d).start())

    turned = back_in[...].reshape(row_slots * blk, width).T

    def backward(s):
        right = jnp.concatenate(
            [vals[inv[t * col_slots + s]] for t in range(row_slots)], axis=0
        )
        total = jnp.dot(turned, right, preferred_element_type=jnp.float32)
        return total.T.astype(jnp.bfloat16)

    def dx_copy(d):
        r = row_at(d)
        return to_row(
            d,
            dx_out.at[pl.ds(r * cap, cap)],
            dx_in.at[pl.ds(r_me * cap, cap)],
            dx_s,
            dx_r,
        )

    def backward_to(d):
        for k in range(cap):
            dx_out[row_at(d) * cap + k] = backward(row_at(d) * cap + k)
        dx_copy(d).start()

    each(n_rows, backward_to)
    for k in range(cap):
        dx_in[r_me * cap + k] = backward(r_me * cap + k)

    each(n_cols, lambda d: wg2_copy(d).wait())
    total = wg_part[0]
    for o in range(1, n_cols):
        total = total + wg_part[o]
    total = total * scale
    wg_out[0] = total
    wg_done[r_me] = total
    each(n_rows, lambda d: wg3_copy(d).start())

    each(n_rows, lambda d: dx_copy(d).wait())
    col_asked = [[col_sm[o, 0, r_me * cap + q] for q in range(cap)] for o in range(n_rows)]
    for k in range(per_dev):
        input_grad[pl.ds(k * blk, blk), :] = total_of(dx_in, col_asked, n_rows, k)
    each(n_rows, lambda d: wg3_copy(d).wait())
    for o in range(n_rows):
        weight_grad[pl.ds(o * piece, piece), :] = wg_done[o]


def on_device(features, out_grad, weight, block_values, block_slot, live_count, row_need, col_need):
    n_rows = lax.axis_size("gr")
    n_cols = lax.axis_size("gc")
    values = block_values[0, 0]
    nzb, blk, _ = values.shape
    local, width = features.shape[2:]
    per_dev = local // blk
    cap = row_need.shape[3]
    col_slots = n_rows * cap
    row_slots = n_cols * cap
    place = jnp.arange(col_slots * row_slots)
    block = jnp.arange(nzb)
    match = (block_slot[0, 0][None, :] == place[:, None]) & (block < live_count[0, 0])[None, :]
    inv = jnp.min(jnp.where(match, block[None, :], nzb), axis=1).astype(jnp.int32)

    def padded(need):
        flat = need.reshape(1, -1)
        return jnp.pad(flat, ((0, 0), (0, -flat.shape[1] % 128)))

    row_meta = padded(row_need)
    col_meta = padded(col_need)
    bf, f32, i32 = jnp.bfloat16, jnp.float32, jnp.int32
    piece = width // n_rows
    dma = pltpu.SemaphoreType.DMA
    vmem = pl.BlockSpec(memory_space=pltpu.VMEM)
    smem = pl.BlockSpec(memory_space=pltpu.SMEM)
    hbm = pl.BlockSpec(memory_space=pl.ANY)
    scale = float(local * n_rows * n_cols) ** (-0.5)
    flops = 4 * nzb * blk * blk * width
    activated, weight_grad, input_grad = pl.pallas_call(
        functools.partial(kernel, n_rows, n_cols, cap, scale),
        out_shape=(
            jax.ShapeDtypeStruct((local, width), bf),
            jax.ShapeDtypeStruct((width, width), f32),
            jax.ShapeDtypeStruct((local, width), bf),
        ),
        in_specs=[smem, smem, vmem, vmem, hbm, vmem, vmem, hbm],
        out_specs=(vmem, vmem, vmem),
        scratch_shapes=[
            pltpu.VMEM((nzb + 1, blk, blk), bf),
            pltpu.VMEM((n_rows * per_dev, blk, width), bf),
            pltpu.VMEM((col_slots * blk, width), bf),
            pltpu.VMEM((row_slots, blk, width), bf),
            pltpu.VMEM((row_slots + 1, blk, width), bf),
            pltpu.VMEM((local, width), bf),
            pltpu.VMEM((per_dev, blk, width), bf),
            pltpu.VMEM((row_slots, blk, width), bf),
            pltpu.VMEM((row_slots, blk, width), bf),
            pltpu.VMEM((col_slots, blk, width), bf),
            pltpu.VMEM((col_slots + 1, blk, width), bf),
            pltpu.VMEM((n_cols,) + row_meta.shape, i32),
            pltpu.VMEM((n_rows,) + col_meta.shape, i32),
            pltpu.SMEM((n_cols,) + row_meta.shape, i32),
            pltpu.SMEM((n_rows,) + col_meta.shape, i32),
            pltpu.VMEM((n_rows, piece, width), f32),
            pltpu.VMEM((n_rows, piece, width), f32),
            pltpu.VMEM((piece, width), f32),
            pltpu.VMEM((n_cols, piece, width), f32),
            pltpu.VMEM((n_rows, piece, width), f32),
            dma((4,)),
            dma((n_cols,)),
            dma((n_cols,)),
            dma((n_rows,)),
            dma((n_rows,)),
            dma((n_rows,)),
            dma((n_rows,)),
            dma((n_cols,)),
            dma((n_cols,)),
            dma((n_cols,)),
            dma((n_cols,)),
            dma((n_rows,)),
            dma((n_rows,)),
            dma((n_rows,)),
            dma((n_rows,)),
            dma((n_cols,)),
            dma((n_cols,)),
            dma((n_rows,)),
            dma((n_rows,)),
        ],
        compiler_params=pltpu.CompilerParams(
            collective_id=0, has_side_effects=True, vmem_limit_bytes=48 * 2**20
        ),
        cost_estimate=pl.CostEstimate(
            flops=flops, bytes_accessed=values.size * 2, transcendentals=0
        ),
    )(
        inv,
        col_need[0, 0],
        row_meta,
        col_meta,
        features.reshape(per_dev, blk, width),
        out_grad.reshape(local, width),
        weight,
        values,
    )
    shape = (1, 1, local, width)
    return activated.reshape(shape), weight_grad, input_grad.reshape(shape)


def solution(mesh):
    placed = (
        P("gc", "gr", None, None),
        P("gr", "gc", None, None),
        P(),
        P("gr", "gc", None, None, None),
        P("gr", "gc", None),
        P("gr", "gc"),
        P("gr", "gc", None, None),
        P("gr", "gc", None, None),
    )
    return jax.shard_map(
        on_device,
        mesh=mesh,
        in_specs=placed,
        out_specs=(P("gr", "gc", None, None), P(), P("gc", "gr", None, None)),
        check_vma=False,
    )
```

```python
import functools

import jax
import jax.numpy as jnp
from jax import lax
from jax.experimental import pallas as pl
from jax.experimental.pallas import tpu as pltpu
from jax.sharding import PartitionSpec as P

MESH = pl.DeviceIdType.MESH


def kernel(n_rows, n_cols, cap, scale, *refs):
    (
        live,
        col_own,
        slot,
        row_need,
        col_need,
        features,
        out_grad,
        weight,
        values,
        activated,
        weight_grad,
        input_grad,
    ) = refs[:12]
    (
        vals,
        w_vm,
        up_vm,
        slot_vm,
        inv_vm,
        inv_sm,
        acc,
        part_out,
        part_in,
        agg,
        back,
        back_out,
        back_in,
        dx_acc,
        dx_out,
        dx_in,
        row_vm,
        col_vm,
        row_sm,
        col_sm,
        wg_out,
        wg_in,
        wg_piece,
        wg_part,
        wg_sum,
        wg_done,
        local_sem,
        row_meta_s,
        row_meta_r,
        col_meta_s,
        col_meta_r,
        feat_s,
        feat_r,
        relay_s,
        relay_r,
        part_s,
        part_r,
        back_s,
        back_r,
        dx_s,
        dx_r,
        wg1_s,
        wg1_r,
        wg2_s,
        wg2_r,
        wg3_s,
        wg3_r,
    ) = refs[12:59]
    boxes = refs[59:]
    half = n_rows // 2
    direct, relayed = boxes[:half], boxes[half:]
    r_me, c_me = lax.axis_index("gr"), lax.axis_index("gc")
    r_other = r_me + 1 - 2 * lax.rem(r_me, 2)
    nzb, blk, _ = values.shape
    per_dev, _, width = features.shape
    col_slots, row_slots = n_rows * cap, n_cols * cap
    lanes = inv_vm.shape[1]

    def row_at(d):
        return lax.rem(r_me + d, n_rows)

    def col_at(d):
        return lax.rem(c_me + d, n_cols)

    def remote(axis, to, src, dst, send, recv):
        return pltpu.make_async_remote_copy(
            src_ref=src,
            dst_ref=dst,
            send_sem=send,
            recv_sem=recv,
            device_id={axis: to},
            device_id_type=MESH,
        )

    def to_row(d, src, dst, send, recv):
        return remote("gr", row_at(d), src, dst, send.at[d], recv.at[d])

    def to_col(d, src, dst, send, recv):
        return remote("gc", col_at(d), src, dst, send.at[d], recv.at[d])

    def each(n, body, start=1):
        def step(d, carry):
            body(d)
            return carry

        lax.fori_loop(start, n, step, 0)

    def inv_at(t, s):
        p = t * col_slots + s
        return inv_sm[lax.div(p, lanes), lax.rem(p, lanes)]

    loads = [
        pltpu.make_async_copy(src, dst, local_sem.at[n])
        for n, (src, dst) in enumerate(
            (
                (slot, slot_vm),
                (features, direct[0]),
                (values, vals.at[pl.ds(0, nzb)]),
                (row_need, row_vm.at[c_me]),
                (col_need, col_vm.at[r_me]),
                (weight, w_vm),
                (out_grad, up_vm),
            )
        )
    ]
    for load in loads:
        load.start()

    barrier = pltpu.get_barrier_semaphore()

    def greet_row(d):
        pl.semaphore_signal(barrier, inc=1, device_id={"gr": row_at(d)}, device_id_type=MESH)

    def greet_col(d):
        pl.semaphore_signal(barrier, inc=1, device_id={"gc": col_at(d)}, device_id_type=MESH)

    each(n_rows, greet_row)
    each(n_cols, greet_col)

    vals[nzb] = jnp.zeros((blk, blk), jnp.bfloat16)
    part_in[row_slots] = jnp.zeros((blk, width), jnp.bfloat16)
    dx_in[col_slots] = jnp.zeros((blk, width), jnp.bfloat16)
    pl.semaphore_wait(barrier, n_rows + n_cols - 2)

    def feat_copy(j):
        return remote(
            "gr", row_at(2 * j), features, direct[j], feat_s.at[j], feat_r.at[j]
        )

    def relay_copy(j):
        src = features if j == 0 else direct[j]
        return remote("gr", r_other, src, relayed[j], relay_s.at[j], relay_r.at[j])

    def row_meta_copy(d):
        return to_col(d, row_need, row_vm.at[c_me], row_meta_s, row_meta_r)

    def col_meta_copy(d):
        return to_row(d, col_need, col_vm.at[r_me], col_meta_s, col_meta_r)

    for j in range(1, half):
        feat_copy(j).start()
    relay_copy(0).start()
    each(n_cols, lambda d: row_meta_copy(d).start())
    each(n_rows, lambda d: col_meta_copy(d).start())

    loads[0].wait()
    turned_slot = jnp.broadcast_to(slot_vm[...], (lanes, nzb)).T
    block = lax.broadcasted_iota(jnp.int32, (nzb, lanes), 0)
    place = lax.broadcasted_iota(jnp.int32, (nzb, lanes), 1)
    alive = block < live[0, 0]
    for q in range(inv_vm.shape[0]):
        match = alive & (turned_slot == place + q * lanes)
        inv_vm[q : q + 1, :] = jnp.min(jnp.where(match, block, nzb), axis=0, keepdims=True)
    inv_load = pltpu.make_async_copy(inv_vm, inv_sm, local_sem.at[7])
    inv_load.start()
    inv_load.wait()
    loads[1].wait()
    loads[2].wait()

    group = min(row_slots, 8)

    def forward(box, owner, first=False):
        right = jnp.concatenate([box[col_own[c, owner]] for c in range(cap)], axis=0)

        def step(g):
            for q in range(group):
                t = g * group + q
                left = jnp.concatenate(
                    [vals[inv_at(t, owner * cap + c)] for c in range(cap)], axis=1
                )
                term = jnp.dot(left, right, preferred_element_type=jnp.float32)
                acc[t] = term if first else acc[t] + term

        if group == row_slots:
            step(0)
        else:
            each(row_slots // group, step, 0)

    forward(direct[0], r_me, True)
    relay_copy(0).wait()
    forward(relayed[0], r_other)
    for j in range(1, half):
        feat_copy(j).wait()
        relay_copy(j).start()
        forward(direct[j], lax.rem(r_me - 2 * j + n_rows, n_rows))
        if j > 1:
            relay_copy(j - 1).wait()
            forward(relayed[j - 1], lax.rem(r_other - 2 * (j - 1) + n_rows, n_rows))
    if half > 1:
        relay_copy(half - 1).wait()
        forward(relayed[half - 1], lax.rem(r_other - 2 * (half - 1) + n_rows, n_rows))

    def part_copy(d):
        src = part_out.at[pl.ds(col_at(d) * cap, cap)]
        return to_col(d, src, part_in.at[pl.ds(c_me * cap, cap)], part_s, part_r)

    def part_to(d):
        for k in range(cap):
            t = col_at(d) * cap + k
            part_out[t] = acc[t].astype(jnp.bfloat16)
        part_copy(d).start()

    each(n_cols, part_to)
    for k in range(cap):
        part_in[c_me * cap + k] = acc[c_me * cap + k].astype(jnp.bfloat16)

    loads[3].wait()
    loads[4].wait()
    each(n_cols, lambda d: row_meta_copy(d).wait())
    each(n_rows, lambda d: col_meta_copy(d).wait())
    row_load = pltpu.make_async_copy(row_vm, row_sm, local_sem.at[8])
    col_load = pltpu.make_async_copy(col_vm, col_sm, local_sem.at[9])
    row_load.start()
    col_load.start()
    loads[5].wait()
    loads[6].wait()
    row_load.wait()
    col_load.wait()
    each(n_cols, lambda d: part_copy(d).wait())

    def total_of(ref, asked, n, k):
        total = jnp.zeros((blk, width), jnp.float32)
        for o in range(n):
            at = n * cap
            for q in range(cap):
                at = jnp.where(asked[o][q] == k, o * cap + q, at)
            total = total + ref[at].astype(jnp.float32)
        return total.astype(jnp.bfloat16)

    row_asked = [[row_sm[o, q, c_me] for q in range(cap)] for o in range(n_cols)]
    for k in range(per_dev):
        agg[pl.ds(k * blk, blk), :] = total_of(part_in, row_asked, n_cols, k)
    held = agg[...]
    pre = jnp.dot(held, w_vm[...], preferred_element_type=jnp.float32)
    sig = jax.nn.sigmoid(pre)
    upstream = up_vm[...].astype(jnp.float32)
    grad_pre = (upstream * sig * (1.0 + pre * (1.0 - sig))).astype(jnp.bfloat16)
    rows = lax.dot_general(
        grad_pre, w_vm[...], (((1,), (1,)), ((), ())), preferred_element_type=jnp.float32
    ).astype(jnp.bfloat16)
    for k in range(per_dev):
        back[k] = rows[k * blk : (k + 1) * blk]

    def back_copy(d):
        src = back_out.at[pl.ds(col_at(d) * cap, cap)]
        return to_col(d, src, back_in.at[pl.ds(c_me * cap, cap)], back_s, back_r)

    def back_to(d):
        c = col_at(d)
        for k in range(cap):
            back_out[c * cap + k] = back[row_sm[c, k, c_me]]
        back_copy(d).start()

    each(n_cols, back_to)
    for k in range(cap):
        back_in[c_me * cap + k] = back[row_sm[c_me, k, c_me]]
    activated[...] = (pre * sig).astype(jnp.bfloat16)

    term = lax.dot_general(
        held, grad_pre, (((0,), (0,)), ((), ())), preferred_element_type=jnp.float32
    )
    piece = term.shape[0] // n_rows
    for o in range(n_rows):
        wg_out[o] = term[o * piece : (o + 1) * piece]
    wg_in[r_me] = wg_out[r_me]

    def wg1_copy(d):
        return to_row(d, wg_out.at[row_at(d)], wg_in.at[r_me], wg1_s, wg1_r)

    def wg2_copy(d):
        return to_col(d, wg_piece, wg_part.at[c_me], wg2_s, wg2_r)

    def wg3_copy(d):
        return to_row(d, wg_sum, wg_done.at[r_me], wg3_s, wg3_r)

    each(n_rows, lambda d: wg1_copy(d).start())

    def backward(turned, c, r):
        right = jnp.concatenate(
            [
                jnp.concatenate(
                    [vals[inv_at(c * cap + q, r * cap + k)] for k in range(cap)], axis=1
                )
                for q in range(cap)
            ],
            axis=0,
        )
        return jnp.dot(turned, right, preferred_element_type=jnp.float32)

    def turn(c):
        return back_in[pl.ds(c * cap, cap)].reshape(cap * blk, width).T

    group_r = min(n_rows, 8)

    def backward_all(c, first=False):
        turned = turn(c)

        def step(g):
            for q in range(group_r):
                r = g * group_r + q
                total = backward(turned, c, r)
                dx_acc[r] = total if first else dx_acc[r] + total

        if group_r == n_rows:
            step(0)
        else:
            each(n_rows // group_r, step, 0)

    backward_all(c_me, True)

    each(n_rows, lambda d: wg1_copy(d).wait())
    total = wg_in[0]
    for o in range(1, n_rows):
        total = total + wg_in[o]
    wg_piece[...] = total
    wg_part[c_me] = total
    each(n_cols, lambda d: wg2_copy(d).start())

    def source(d):
        return lax.rem(c_me - d + n_cols, n_cols)

    def backward_from(d):
        back_copy(d).wait()
        backward_all(source(d))

    each(n_cols - 1, backward_from)
    back_copy(n_cols - 1).wait()
    last = source(n_cols - 1)
    turned = turn(last)

    def dx_copy(d):
        src = dx_out.at[pl.ds(row_at(d) * cap, cap)]
        return to_row(d, src, dx_in.at[pl.ds(r_me * cap, cap)], dx_s, dx_r)

    def backward_last(r, ref):
        total = dx_acc[r] + backward(turned, last, r)
        for k in range(cap):
            ref[r * cap + k] = total[:, k * blk : (k + 1) * blk].T.astype(jnp.bfloat16)

    def backward_to(d):
        backward_last(row_at(d), dx_out)
        dx_copy(d).start()

    each(n_rows, backward_to)
    backward_last(r_me, dx_in)

    each(n_cols, lambda d: wg2_copy(d).wait())
    total = wg_part[0]
    for o in range(1, n_cols):
        total = total + wg_part[o]
    total = total * scale
    wg_sum[...] = total
    wg_done[r_me] = total
    each(n_rows, lambda d: wg3_copy(d).start())

    each(n_rows, lambda d: dx_copy(d).wait())
    col_asked = [[col_sm[o, q, r_me] for q in range(cap)] for o in range(n_rows)]
    for k in range(per_dev):
        input_grad[pl.ds(k * blk, blk), :] = total_of(dx_in, col_asked, n_rows, k)
    each(n_rows, lambda d: wg3_copy(d).wait())
    for o in range(n_rows):
        weight_grad[pl.ds(o * piece, piece), :] = wg_done[o]


def on_device(features, out_grad, weight, block_values, block_slot, live_count, row_need, col_need):
    n_rows = lax.axis_size("gr")
    n_cols = lax.axis_size("gc")
    values = block_values[0, 0]
    nzb, blk, _ = values.shape
    local, width = features.shape[2:]
    per_dev = local // blk
    cap = row_need.shape[3]
    col_slots = n_rows * cap
    row_slots = n_cols * cap
    bf, f32, i32 = jnp.bfloat16, jnp.float32, jnp.int32
    piece = width // n_rows
    places = col_slots * row_slots
    half = n_rows // 2
    dma = pltpu.SemaphoreType.DMA
    vmem = pl.BlockSpec(memory_space=pltpu.VMEM)
    smem = pl.BlockSpec(memory_space=pltpu.SMEM)
    hbm = pl.BlockSpec(memory_space=pltpu.HBM)
    scale = float(local * n_rows * n_cols) ** (-0.5)
    flops = 4 * nzb * blk * blk * width
    box = pltpu.VMEM((per_dev, blk, width), bf)
    rows_dma, cols_dma, half_dma = dma((n_rows,)), dma((n_cols,)), dma((half,))
    activated, weight_grad, input_grad = pl.pallas_call(
        functools.partial(kernel, n_rows, n_cols, cap, scale),
        out_shape=(
            jax.ShapeDtypeStruct((local, width), bf),
            jax.ShapeDtypeStruct((width, width), f32),
            jax.ShapeDtypeStruct((local, width), bf),
        ),
        in_specs=[smem, smem] + [hbm] * 7,
        out_specs=(vmem, vmem, vmem),
        scratch_shapes=[
            pltpu.VMEM((nzb + 1, blk, blk), bf),
            pltpu.VMEM((width, width), bf),
            pltpu.VMEM((local, width), bf),
            pltpu.VMEM((1, nzb), i32),
            pltpu.VMEM((places // 128, 128), i32),
            pltpu.SMEM((places // 128, 128), i32),
            pltpu.VMEM((row_slots, blk, width), f32),
            pltpu.VMEM((row_slots, blk, width), bf),
            pltpu.VMEM((row_slots + 1, blk, width), bf),
            pltpu.VMEM((local, width), bf),
            pltpu.VMEM((per_dev, blk, width), bf),
            pltpu.VMEM((row_slots, blk, width), bf),
            pltpu.VMEM((row_slots, blk, width), bf),
            pltpu.VMEM((n_rows, width, cap * blk), f32),
            pltpu.VMEM((col_slots, blk, width), bf),
            pltpu.VMEM((col_slots + 1, blk, width), bf),
            pltpu.VMEM((n_cols, cap, n_cols), i32),
            pltpu.VMEM((n_rows, cap, n_rows), i32),
            pltpu.SMEM((n_cols, cap, n_cols), i32),
            pltpu.SMEM((n_rows, cap, n_rows), i32),
            pltpu.VMEM((n_rows, piece, width), f32),
            pltpu.VMEM((n_rows, piece, width), f32),
            pltpu.VMEM((piece, width), f32),
            pltpu.VMEM((n_cols, piece, width), f32),
            pltpu.VMEM((piece, width), f32),
            pltpu.VMEM((n_rows, piece, width), f32),
            dma((10,)),
            cols_dma,
            cols_dma,
            rows_dma,
            rows_dma,
            half_dma,
            half_dma,
            half_dma,
            half_dma,
            cols_dma,
            cols_dma,
            cols_dma,
            cols_dma,
            rows_dma,
            rows_dma,
            rows_dma,
            rows_dma,
            cols_dma,
            cols_dma,
            rows_dma,
            rows_dma,
        ]
        + [box] * (2 * half),
        compiler_params=pltpu.CompilerParams(
            collective_id=0, has_side_effects=True, vmem_limit_bytes=48 * 2**20
        ),
        cost_estimate=pl.CostEstimate(
            flops=flops, bytes_accessed=values.size * 2, transcendentals=0
        ),
    )(
        live_count,
        col_need[0, 0].T,
        block_slot.reshape(1, nzb),
        row_need[0, 0].T,
        col_need[0, 0].T,
        features.reshape(per_dev, blk, width),
        out_grad.reshape(local, width),
        weight,
        values,
    )
    shape = (1, 1, local, width)
    return activated.reshape(shape), weight_grad, input_grad.reshape(shape)


def solution(mesh):
    placed = (
        P("gc", "gr", None, None),
        P("gr", "gc", None, None),
        P(),
        P("gr", "gc", None, None, None),
        P("gr", "gc", None),
        P("gr", "gc"),
        P("gr", "gc", None, None),
        P("gr", "gc", None, None),
    )
    return jax.shard_map(
        on_device,
        mesh=mesh,
        in_specs=placed,
        out_specs=(P("gr", "gc", None, None), P(), P("gc", "gr", None, None)),
        check_vma=False,
    )
```

```python
import functools

import jax
import jax.numpy as jnp
from jax import lax
from jax.experimental import pallas as pl
from jax.experimental.pallas import tpu as pltpu
from jax.sharding import PartitionSpec as P

MESH = pl.DeviceIdType.MESH


def kernel(n_rows, n_cols, cap, scale, *refs):
    (
        live,
        col_own,
        slot,
        row_need,
        col_need,
        features,
        out_grad,
        weight,
        values,
        activated,
        weight_grad,
        input_grad,
    ) = refs[:12]
    (
        vals,
        w_vm,
        up_vm,
        slot_vm,
        inv_vm,
        inv_sm,
        acc,
        part_out,
        part_in,
        agg,
        back,
        back_out,
        back_in,
        dx_acc,
        dx_out,
        dx_in,
        row_vm,
        col_vm,
        row_sm,
        col_sm,
        wg_out,
        wg_in,
        wg_piece,
        wg_part,
        wg_sum,
        wg_done,
        local_sem,
        row_meta_s,
        row_meta_r,
        col_meta_s,
        col_meta_r,
        feat_s,
        feat_r,
        relay_s,
        relay_r,
        part_s,
        part_r,
        back_s,
        back_r,
        dx_s,
        dx_r,
        wg1_s,
        wg1_r,
        wg2_s,
        wg2_r,
        wg3_s,
        wg3_r,
    ) = refs[12:59]
    boxes = refs[59:]
    half = n_rows // 2
    direct, relayed = boxes[:half], boxes[half:]
    r_me, c_me = lax.axis_index("gr"), lax.axis_index("gc")
    r_other = r_me + 1 - 2 * lax.rem(r_me, 2)
    nzb, blk, _ = values.shape
    per_dev, _, width = features.shape
    col_slots, row_slots = n_rows * cap, n_cols * cap
    lanes = inv_vm.shape[1]

    def row_at(d):
        return lax.rem(r_me + d, n_rows)

    def col_at(d):
        return lax.rem(c_me + d, n_cols)

    def remote(axis, to, src, dst, send, recv):
        return pltpu.make_async_remote_copy(
            src_ref=src,
            dst_ref=dst,
            send_sem=send,
            recv_sem=recv,
            device_id={axis: to},
            device_id_type=MESH,
        )

    def to_row(d, src, dst, send, recv):
        return remote("gr", row_at(d), src, dst, send.at[d], recv.at[d])

    def to_col(d, src, dst, send, recv):
        return remote("gc", col_at(d), src, dst, send.at[d], recv.at[d])

    def each(n, body, start=1):
        def step(d, carry):
            body(d)
            return carry

        lax.fori_loop(start, n, step, 0)

    def inv_at(t, s):
        p = t * col_slots + s
        return inv_sm[lax.div(p, lanes), lax.rem(p, lanes)]

    loads = [
        pltpu.make_async_copy(src, dst, local_sem.at[n])
        for n, (src, dst) in enumerate(
            (
                (slot, slot_vm),
                (features, direct[0]),
                (values, vals.at[pl.ds(0, nzb)]),
                (row_need, row_vm.at[c_me]),
                (col_need, col_vm.at[r_me]),
                (weight, w_vm),
                (out_grad, up_vm),
            )
        )
    ]
    for load in loads:
        load.start()

    barrier = pltpu.get_barrier_semaphore()

    def greet_row(d):
        pl.semaphore_signal(barrier, inc=1, device_id={"gr": row_at(d)}, device_id_type=MESH)

    def greet_col(d):
        pl.semaphore_signal(barrier, inc=1, device_id={"gc": col_at(d)}, device_id_type=MESH)

    each(n_rows, greet_row)
    each(n_cols, greet_col)

    vals[nzb] = jnp.zeros((blk, blk), jnp.bfloat16)
    part_in[row_slots] = jnp.zeros((blk, width), jnp.bfloat16)
    dx_in[col_slots] = jnp.zeros((blk, width), jnp.bfloat16)

    loads[0].wait()
    turned_slot = jnp.broadcast_to(slot_vm[...], (lanes, nzb)).T
    block = lax.broadcasted_iota(jnp.int32, (nzb, lanes), 0)
    place = lax.broadcasted_iota(jnp.int32, (nzb, lanes), 1)
    alive = block < live[0, 0]
    for q in range(inv_vm.shape[0]):
        match = alive & (turned_slot == place + q * lanes)
        inv_vm[q : q + 1, :] = jnp.min(jnp.where(match, block, nzb), axis=0, keepdims=True)
    inv_load = pltpu.make_async_copy(inv_vm, inv_sm, local_sem.at[7])
    inv_load.start()
    inv_load.wait()
    loads[1].wait()
    loads[2].wait()

    group = min(row_slots, 8)

    def forward(box, owner, first=False):
        right = jnp.concatenate([box[col_own[c, owner]] for c in range(cap)], axis=0)

        def step(g):
            for q in range(group):
                t = g * group + q
                left = jnp.concatenate(
                    [vals[inv_at(t, owner * cap + c)] for c in range(cap)], axis=1
                )
                term = jnp.dot(left, right, preferred_element_type=jnp.float32)
                acc[t] = term if first else acc[t] + term

        if group == row_slots:
            step(0)
        else:
            each(row_slots // group, step, 0)

    forward(direct[0], r_me, True)

    def feat_copy(j):
        return remote(
            "gr", row_at(2 * j), features, direct[j], feat_s.at[j], feat_r.at[j]
        )

    def relay_copy(j):
        src = features if j == 0 else direct[j]
        return remote("gr", r_other, src, relayed[j], relay_s.at[j], relay_r.at[j])

    def row_meta_copy(d):
        return to_col(d, row_need, row_vm.at[c_me], row_meta_s, row_meta_r)

    def col_meta_copy(d):
        return to_row(d, col_need, col_vm.at[r_me], col_meta_s, col_meta_r)

    pl.semaphore_wait(barrier, n_rows + n_cols - 2)
    for j in range(1, half):
        feat_copy(j).start()
    relay_copy(0).start()
    each(n_cols, lambda d: row_meta_copy(d).start())
    each(n_rows, lambda d: col_meta_copy(d).start())

    relay_copy(0).wait()
    forward(relayed[0], r_other)
    for j in range(1, half):
        feat_copy(j).wait()
        relay_copy(j).start()
        forward(direct[j], lax.rem(r_me - 2 * j + n_rows, n_rows))
        if j > 1:
            relay_copy(j - 1).wait()
            forward(relayed[j - 1], lax.rem(r_other - 2 * (j - 1) + n_rows, n_rows))
    if half > 1:
        relay_copy(half - 1).wait()
        forward(relayed[half - 1], lax.rem(r_other - 2 * (half - 1) + n_rows, n_rows))

    def part_copy(d):
        src = part_out.at[pl.ds(col_at(d) * cap, cap)]
        return to_col(d, src, part_in.at[pl.ds(c_me * cap, cap)], part_s, part_r)

    def part_to(d):
        for k in range(cap):
            t = col_at(d) * cap + k
            part_out[t] = acc[t].astype(jnp.bfloat16)
        part_copy(d).start()

    each(n_cols, part_to)
    for k in range(cap):
        part_in[c_me * cap + k] = acc[c_me * cap + k].astype(jnp.bfloat16)

    loads[3].wait()
    loads[4].wait()
    each(n_cols, lambda d: row_meta_copy(d).wait())
    each(n_rows, lambda d: col_meta_copy(d).wait())
    row_load = pltpu.make_async_copy(row_vm, row_sm, local_sem.at[8])
    col_load = pltpu.make_async_copy(col_vm, col_sm, local_sem.at[9])
    row_load.start()
    col_load.start()
    loads[5].wait()
    loads[6].wait()
    row_load.wait()
    col_load.wait()
    each(n_cols, lambda d: part_copy(d).wait())

    def total_of(ref, asked, n, k):
        total = jnp.zeros((blk, width), jnp.float32)
        for o in range(n):
            at = n * cap
            for q in range(cap):
                at = jnp.where(asked[o][q] == k, o * cap + q, at)
            total = total + ref[at].astype(jnp.float32)
        return total.astype(jnp.bfloat16)

    row_asked = [[row_sm[o, q, c_me] for q in range(cap)] for o in range(n_cols)]
    for k in range(per_dev):
        agg[pl.ds(k * blk, blk), :] = total_of(part_in, row_asked, n_cols, k)
    held = agg[...]
    pre = jnp.dot(held, w_vm[...], preferred_element_type=jnp.float32)
    sig = jax.nn.sigmoid(pre)
    upstream = up_vm[...].astype(jnp.float32)
    grad_pre = (upstream * sig * (1.0 + pre * (1.0 - sig))).astype(jnp.bfloat16)
    rows = lax.dot_general(
        grad_pre, w_vm[...], (((1,), (1,)), ((), ())), preferred_element_type=jnp.float32
    ).astype(jnp.bfloat16)
    for k in range(per_dev):
        back[k] = rows[k * blk : (k + 1) * blk]

    def back_copy(d):
        src = back_out.at[pl.ds(col_at(d) * cap, cap)]
        return to_col(d, src, back_in.at[pl.ds(c_me * cap, cap)], back_s, back_r)

    def back_to(d):
        c = col_at(d)
        for k in range(cap):
            back_out[c * cap + k] = back[row_sm[c, k, c_me]]
        back_copy(d).start()

    each(n_cols, back_to)
    for k in range(cap):
        back_in[c_me * cap + k] = back[row_sm[c_me, k, c_me]]
    activated[...] = (pre * sig).astype(jnp.bfloat16)

    term = lax.dot_general(
        held, grad_pre, (((0,), (0,)), ((), ())), preferred_element_type=jnp.float32
    )
    piece = term.shape[0] // n_rows
    for o in range(n_rows):
        wg_out[o] = term[o * piece : (o + 1) * piece]
    wg_in[r_me] = wg_out[r_me]

    def wg1_copy(d):
        return to_row(d, wg_out.at[row_at(d)], wg_in.at[r_me], wg1_s, wg1_r)

    def wg2_copy(d):
        return to_col(d, wg_piece, wg_part.at[c_me], wg2_s, wg2_r)

    def wg3_copy(d):
        return to_row(d, wg_sum, wg_done.at[r_me], wg3_s, wg3_r)

    each(n_rows, lambda d: wg1_copy(d).start())

    def backward(turned, c, r):
        right = jnp.concatenate(
            [
                jnp.concatenate(
                    [vals[inv_at(c * cap + q, r * cap + k)] for k in range(cap)], axis=1
                )
                for q in range(cap)
            ],
            axis=0,
        )
        return jnp.dot(turned, right, preferred_element_type=jnp.float32)

    def turn(c):
        return back_in[pl.ds(c * cap, cap)].reshape(cap * blk, width).T

    group_r = min(n_rows, 8)

    def backward_all(c, first=False):
        turned = turn(c)

        def step(g):
            for q in range(group_r):
                r = g * group_r + q
                total = backward(turned, c, r)
                dx_acc[r] = total if first else dx_acc[r] + total

        if group_r == n_rows:
            step(0)
        else:
            each(n_rows // group_r, step, 0)

    backward_all(c_me, True)

    each(n_rows, lambda d: wg1_copy(d).wait())
    total = wg_in[0]
    for o in range(1, n_rows):
        total = total + wg_in[o]
    wg_piece[...] = total
    wg_part[c_me] = total
    each(n_cols, lambda d: wg2_copy(d).start())

    def source(d):
        return lax.rem(c_me - d + n_cols, n_cols)

    def backward_from(d):
        back_copy(d).wait()
        backward_all(source(d))

    each(n_cols - 1, backward_from)
    back_copy(n_cols - 1).wait()
    last = source(n_cols - 1)
    turned = turn(last)

    def dx_copy(d):
        src = dx_out.at[pl.ds(row_at(d) * cap, cap)]
        return to_row(d, src, dx_in.at[pl.ds(r_me * cap, cap)], dx_s, dx_r)

    def backward_last(r, ref):
        total = dx_acc[r] + backward(turned, last, r)
        for k in range(cap):
            ref[r * cap + k] = total[:, k * blk : (k + 1) * blk].T.astype(jnp.bfloat16)

    def backward_to(d):
        backward_last(row_at(d), dx_out)
        dx_copy(d).start()

    each(n_rows, backward_to)
    backward_last(r_me, dx_in)

    each(n_cols, lambda d: wg2_copy(d).wait())
    total = wg_part[0]
    for o in range(1, n_cols):
        total = total + wg_part[o]
    total = total * scale
    wg_sum[...] = total
    wg_done[r_me] = total
    each(n_rows, lambda d: wg3_copy(d).start())

    each(n_rows, lambda d: dx_copy(d).wait())
    col_asked = [[col_sm[o, q, r_me] for q in range(cap)] for o in range(n_rows)]
    for k in range(per_dev):
        input_grad[pl.ds(k * blk, blk), :] = total_of(dx_in, col_asked, n_rows, k)
    each(n_rows, lambda d: wg3_copy(d).wait())
    for o in range(n_rows):
        weight_grad[pl.ds(o * piece, piece), :] = wg_done[o]


def hand_over(n, *refs):
    srcs, dsts, boxes, sem = refs[:n], refs[n : 2 * n], refs[2 * n : 3 * n], refs[3 * n]
    inward = [pltpu.make_async_copy(srcs[k], boxes[k], sem.at[k]) for k in range(n)]
    outward = [pltpu.make_async_copy(boxes[k], dsts[k], sem.at[n + k]) for k in range(n)]
    for copy in inward:
        copy.start()
    for k in range(n):
        inward[k].wait()
        outward[k].start()
    for copy in outward:
        copy.wait()


def on_device(features, out_grad, weight, block_values, block_slot, live_count, row_need, col_need):
    n_rows = lax.axis_size("gr")
    n_cols = lax.axis_size("gc")
    values = block_values[0, 0]
    nzb, blk, _ = values.shape
    local, width = features.shape[2:]
    per_dev = local // blk
    cap = row_need.shape[3]
    col_slots = n_rows * cap
    row_slots = n_cols * cap
    bf, f32, i32 = jnp.bfloat16, jnp.float32, jnp.int32
    piece = width // n_rows
    places = col_slots * row_slots
    half = n_rows // 2
    dma = pltpu.SemaphoreType.DMA
    vmem = pl.BlockSpec(memory_space=pltpu.VMEM)
    smem = pl.BlockSpec(memory_space=pltpu.SMEM)
    hbm = pl.BlockSpec(memory_space=pltpu.HBM)
    scale = float(local * n_rows * n_cols) ** (-0.5)
    flops = 4 * nzb * blk * blk * width
    box = pltpu.VMEM((per_dev, blk, width), bf)
    rows_dma, cols_dma, half_dma = dma((n_rows,)), dma((n_cols,)), dma((half,))
    activated, weight_grad, input_grad = pl.pallas_call(
        functools.partial(kernel, n_rows, n_cols, cap, scale),
        out_shape=(
            jax.ShapeDtypeStruct((local, width), bf),
            jax.ShapeDtypeStruct((width, width), f32),
            jax.ShapeDtypeStruct((local, width), bf),
        ),
        in_specs=[smem, smem] + [hbm] * 7,
        out_specs=(vmem, vmem, vmem),
        scratch_shapes=[
            pltpu.VMEM((nzb + 1, blk, blk), bf),
            pltpu.VMEM((width, width), bf),
            pltpu.VMEM((local, width), bf),
            pltpu.VMEM((1, nzb), i32),
            pltpu.VMEM((places // 128, 128), i32),
            pltpu.SMEM((places // 128, 128), i32),
            pltpu.VMEM((row_slots, blk, width), f32),
            pltpu.VMEM((row_slots, blk, width), bf),
            pltpu.VMEM((row_slots + 1, blk, width), bf),
            pltpu.VMEM((local, width), bf),
            pltpu.VMEM((per_dev, blk, width), bf),
            pltpu.VMEM((row_slots, blk, width), bf),
            pltpu.VMEM((row_slots, blk, width), bf),
            pltpu.VMEM((n_rows, width, cap * blk), f32),
            pltpu.VMEM((col_slots, blk, width), bf),
            pltpu.VMEM((col_slots + 1, blk, width), bf),
            pltpu.VMEM((n_cols, cap, n_cols), i32),
            pltpu.VMEM((n_rows, cap, n_rows), i32),
            pltpu.SMEM((n_cols, cap, n_cols), i32),
            pltpu.SMEM((n_rows, cap, n_rows), i32),
            pltpu.VMEM((n_rows, piece, width), f32),
            pltpu.VMEM((n_rows, piece, width), f32),
            pltpu.VMEM((piece, width), f32),
            pltpu.VMEM((n_cols, piece, width), f32),
            pltpu.VMEM((piece, width), f32),
            pltpu.VMEM((n_rows, piece, width), f32),
            dma((10,)),
            cols_dma,
            cols_dma,
            rows_dma,
            rows_dma,
            half_dma,
            half_dma,
            half_dma,
            half_dma,
            cols_dma,
            cols_dma,
            cols_dma,
            cols_dma,
            rows_dma,
            rows_dma,
            rows_dma,
            rows_dma,
            cols_dma,
            cols_dma,
            rows_dma,
            rows_dma,
        ]
        + [box] * (2 * half),
        compiler_params=pltpu.CompilerParams(
            collective_id=0, has_side_effects=True, vmem_limit_bytes=60 * 2**20
        ),
        cost_estimate=pl.CostEstimate(
            flops=flops, bytes_accessed=values.size * 2, transcendentals=0
        ),
    )(
        live_count,
        col_need[0, 0].T,
        block_slot.reshape(1, nzb),
        row_need[0, 0].T,
        col_need[0, 0].T,
        features.reshape(per_dev, blk, width),
        out_grad.reshape(local, width),
        weight,
        values,
    )
    anywhere = pl.BlockSpec(memory_space=pl.ANY)
    outs = (activated, weight_grad, input_grad)
    activated, weight_grad, input_grad = pl.pallas_call(
        functools.partial(hand_over, len(outs)),
        out_shape=[jax.ShapeDtypeStruct(o.shape, o.dtype) for o in outs],
        in_specs=[anywhere] * 3,
        out_specs=[anywhere] * 3,
        scratch_shapes=[pltpu.VMEM(o.shape, o.dtype) for o in outs] + [dma((2 * len(outs),))],
    )(*outs)
    shape = (1, 1, local, width)
    return activated.reshape(shape), weight_grad, input_grad.reshape(shape)


def solution(mesh):
    placed = (
        P("gc", "gr", None, None),
        P("gr", "gc", None, None),
        P(),
        P("gr", "gc", None, None, None),
        P("gr", "gc", None),
        P("gr", "gc"),
        P("gr", "gc", None, None),
        P("gr", "gc", None, None),
    )
    return jax.shard_map(
        on_device,
        mesh=mesh,
        in_specs=placed,
        out_specs=(P("gr", "gc", None, None), P(), P("gc", "gr", None, None)),
        check_vma=False,
    )
```
